32 devices in a mesh: dp: 8 (over z, x), ctx: 4 (over y, core).
Axes of the slice: x: 2, y: 2, z: 4, core: 2. Of those that a mesh axis runs over, the one named last changes fastest.
Arguments:
- rollout_rows: bfloat16 [8, 512, 5120], P('dp', 'ctx'), may hold values from -6 to 6
- dest_rank: int32 [8, 512], P('dp', 'ctx'), may hold values from 0 to 7, as said below
- doc_ids: int32 [8, 512], P('dp', 'ctx'), may hold values from 0 to 5, never falling along the last dimension, each value on 1 to 384 neighbouring positions
- advantage: float32 [8, 6], P('dp'), may hold values from -4 to 4
- out_grad: bfloat16 [8, 512, 4096], P('dp', 'ctx'), may hold values from -6 to 6
- q_gain: float32 [128], replicated, may hold values from 0.5 to 2
- k_gain: float32 [128], replicated, may hold values from 0.5 to 2
Outputs:
- attn_out: bfloat16 [8, 512, 4096], P('dp', 'ctx')
- packed_row_gradient: bfloat16 [8, 512, 5120], P('dp', 'ctx')
- q_gain_grad: float32 [128], replicated
- k_gain_grad: float32 [128], replicated
The draws below stay inside these ranges and needn't reach their ends.
Inputs may be any that keep to these rules, and one draw needn't show every extreme that they name: `dest_rank`: at every position the 8 rows there go to 8 different ranks. From one device at most 16 rows go to any one other rank, and exactly 16 to one of them; any number of rows may stay. `doc_ids`: document numbers never fall along a pack; each document has at most 384 positions, one exactly 384.
All inputs are finite; a program needn't handle non-finite values.
Results may differ from the reference program's by a relative error of at most 0.014.
Values may be sent and summed in bfloat16 or wider, within the bound.
A program may use at most 64 MiB of HBM per device.

```python
import math
import jax
import jax.numpy as jnp
import numpy as np
from jax import lax

QUERY_HEADS = 32
KEY_VALUE_HEADS = 4
HEAD_SIZE = 128
TOKENS_PER_PACK = 128
DOCS = 6
SEQ = 512
REACH_BLOCKS = 3
DOC_MOST = 384
CAP = 16
WIDTH = 5120
N_DP = 8
N_CTX = 4


def draw_dest_rank(key, part):
    key = jax.random.fold_in(key, 17)

    def column(col_key):
        heavy_key, pool_key, order_key = jax.random.split(col_key, 3)
        heavy = jax.random.randint(heavy_key, (), 1, N_DP)
        pool_values = jnp.arange((N_DP - 1) * CAP, dtype=jnp.int32) // CAP
        picked = jax.random.permutation(pool_key, pool_values)[:TOKENS_PER_PACK // 2 - CAP]
        shifts = jnp.concatenate([jnp.full((CAP,), heavy, jnp.int32), (heavy + 1 + picked) % N_DP, jnp.zeros((TOKENS_PER_PACK - TOKENS_PER_PACK // 2,), jnp.int32)])
        return shifts[jax.random.permutation(order_key, TOKENS_PER_PACK)]
    shifts = jax.vmap(column)(jax.random.split(key, N_CTX)).reshape(SEQ)
    rank_ids = jnp.arange(N_DP, dtype=jnp.int32)[:, None]
    return ((rank_ids + shifts[None, :]) % N_DP).astype(jnp.int32)


def levels(stream_key, shape, cuts, low, high):
    def one(position, blocks):
        draws = jax.random.uniform(jax.random.fold_in(jax.random.fold_in(stream_key, 6), position), (blocks,), jnp.float32, low / len(cuts), high / len(cuts))
        return jnp.repeat(jnp.exp(draws), shape[position] // blocks).reshape((-1,) + (1,) * (len(shape) - position - 1))

    loudness = one(*cuts[0])
    for cut in cuts[1:]:
        loudness = loudness * one(*cut)
    return loudness


def length_profile(amount, total, most, slope):
    loads = [(1 << 20) // math.isqrt(rank ** slope) + 1 for rank in range(2, amount + 1)]
    spare, given = total - most - (amount - 1), [1] * (amount - 1)
    while spare > 0:
        candidates = [i for i in range(amount - 1) if given[i] < most]
        whole, budget = sum([loads[i] for i in candidates]), spare
        for i in candidates:
            more = min(most - given[i], max(1, budget * loads[i] // whole), spare)
            given[i] = given[i] + more
            spare = spare - more
    return np.array([most] + given)


def ragged_sizes(own_key, count, total, limit, slope):
    if count == 2:
        one = jax.random.randint(own_key, (), max(1, total - limit), min(limit, total - 1) + 1)
        return jnp.stack([one, total - one])
    tallies = jnp.asarray(length_profile(count, total, limit, slope), jnp.int32)
    couples = (count - 1) // 2
    donor, taker = tallies[1:1 + 2 * couples:2], tallies[2:2 + 2 * couples:2]
    margin = jnp.minimum(donor - 1, limit - taker)
    passed = jax.random.randint(jax.random.fold_in(own_key, 1), (couples,), 0, 1 << 20) % (margin + 1)
    tallies = tallies.at[1:1 + 2 * couples:2].set(donor - passed).at[2:2 + 2 * couples:2].set(taker + passed)
    return tallies[jax.random.permutation(jax.random.fold_in(own_key, 2), count)]


def centred(rng, shape, spread, limit, cuts=(), kind=jnp.bfloat16):
    values = spread * jax.random.normal(rng, shape, jnp.float32)
    if cuts:
        values = values * levels(rng, shape, cuts, -0.22, 0.18)
    return jnp.clip(values, -limit, limit).astype(kind)


def setup_inputs(seed: int = 0) -> dict:
    splits = jax.random.split(jax.random.key(seed), 8)
    return {
        "rollout_rows": centred(splits[0], (N_DP, SEQ, WIDTH), 1.0, 6.0, ((0, 8), (1, 4))),
        "dest_rank": draw_dest_rank(jax.random.fold_in(splits[7], 71), 0),
        "doc_ids": jax.vmap(lambda own: jnp.searchsorted(jnp.cumsum(ragged_sizes(own, DOCS, SEQ, DOC_MOST, 1)), jnp.arange(SEQ), side="right"))(jax.random.split(splits[2], N_DP)).reshape((N_DP, SEQ)).astype(jnp.int32),
        "advantage": centred(splits[3], (N_DP, DOCS), 1.0, 4.0, ((0, 8),), jnp.float32),
        "out_grad": centred(splits[4], (N_DP, SEQ, QUERY_HEADS * HEAD_SIZE), 1.0, 6.0, ((0, 8), (1, 4))),
        "q_gain": jnp.clip(jnp.exp(jax.random.uniform(splits[5], (HEAD_SIZE,), jnp.float32, math.log(0.5), math.log(2.0))), 0.5, 2.0),
        "k_gain": jnp.clip(jnp.exp(jax.random.uniform(splits[6], (HEAD_SIZE,), jnp.float32, math.log(0.5), math.log(2.0))), 0.5, 2.0),
    }


epsilon = 1e-06

def rms_scale(values, scaling):
    return values * lax.rsqrt(lax.optimization_barrier(jnp.mean(values * values, axis=-1, keepdims=True)) + epsilon) * scaling

def return_journey(values):
    return lax.optimization_barrier(values.astype(jnp.bfloat16)).astype(jnp.float32)

def widen_precision(blocked):
    pieces = [blocked]
    for distance in range(1, REACH_BLOCKS + 1):
        pieces.append(jnp.concatenate([jnp.zeros_like(blocked[:distance]), blocked[:-distance]], axis=0))
    return jnp.concatenate(pieces, axis=1)

def fold_back(window_gradient):
    window_pieces_list = return_journey(window_gradient.reshape(N_CTX, REACH_BLOCKS + 1, TOKENS_PER_PACK, KEY_VALUE_HEADS, HEAD_SIZE))
    summed_parts = window_pieces_list[:, 0]
    for distance in range(1, REACH_BLOCKS + 1):
        summed_parts = summed_parts + jnp.concatenate([window_pieces_list[distance:, distance], jnp.zeros_like(window_pieces_list[:distance, distance])], axis=0)
    return summed_parts.reshape(N_CTX * TOKENS_PER_PACK, KEY_VALUE_HEADS, HEAD_SIZE)

def pack_window(packed_row_block, pack_docs, pack_adv, pack_grad, q_gain, k_gain):
    query_groups = QUERY_HEADS // KEY_VALUE_HEADS
    sequence_length = N_CTX * TOKENS_PER_PACK
    inverse = HEAD_SIZE ** (-0.5)
    q_raw = packed_row_block[:, :QUERY_HEADS * HEAD_SIZE].astype(jnp.float32).reshape(sequence_length, QUERY_HEADS, HEAD_SIZE)
    key_plain_rows = packed_row_block[:, QUERY_HEADS * HEAD_SIZE:(QUERY_HEADS + KEY_VALUE_HEADS) * HEAD_SIZE].astype(jnp.float32).reshape(sequence_length, KEY_VALUE_HEADS, HEAD_SIZE)
    value_row_block = packed_row_block[:, (QUERY_HEADS + KEY_VALUE_HEADS) * HEAD_SIZE:].reshape(N_CTX, TOKENS_PER_PACK, KEY_VALUE_HEADS, HEAD_SIZE)
    q_normed, q_back = jax.vjp(rms_scale, q_raw, q_gain)
    k_normed, k_back = jax.vjp(rms_scale, key_plain_rows, k_gain)
    query_unit_rows = q_normed.astype(jnp.bfloat16)
    key_unit_rows = k_normed.astype(jnp.bfloat16)
    query_matrix = query_unit_rows.astype(jnp.float32).reshape(N_CTX, TOKENS_PER_PACK, KEY_VALUE_HEADS, query_groups, HEAD_SIZE)
    key_matrix = widen_precision(key_unit_rows.reshape(N_CTX, TOKENS_PER_PACK, KEY_VALUE_HEADS, HEAD_SIZE)).astype(jnp.float32)
    values_win = widen_precision(value_row_block).astype(jnp.float32)
    doc_tags = (pack_docs + 1).reshape(N_CTX, TOKENS_PER_PACK)
    key_tags = widen_precision(doc_tags)
    q_pos = jnp.arange(sequence_length, dtype=jnp.int32).reshape(N_CTX, TOKENS_PER_PACK)
    k_pos = jnp.concatenate([q_pos - distance * TOKENS_PER_PACK for distance in range(REACH_BLOCKS + 1)], axis=1)
    allowed = (doc_tags[:, :, None] == key_tags[:, None, :]) & (k_pos[:, None, :] <= q_pos[:, :, None])
    scores = jnp.einsum('btkgd,bskd->bkgts', query_matrix, key_matrix) * inverse
    weights = jnp.where(allowed[:, None, None], jnp.exp(scores), 0.0)
    totals = lax.optimization_barrier(jnp.sum(weights, axis=-1))
    numerator = jnp.einsum('bkgts,bskd->btkgd', return_journey(weights), values_win)
    attention = (numerator / jnp.transpose(totals, (0, 3, 1, 2))[..., None]).astype(jnp.bfloat16)
    doc_hot = (pack_docs[:, None] == jnp.arange(DOCS, dtype=jnp.int32)[None, :]).astype(jnp.float32)
    adv_tok = lax.optimization_barrier(jnp.sum(doc_hot * pack_adv[None, :], axis=1))
    output_gradient = (pack_grad.astype(jnp.float32) * adv_tok[:, None]).astype(jnp.bfloat16)
    output_gradient_wide = output_gradient.astype(jnp.float32).reshape(N_CTX, TOKENS_PER_PACK, KEY_VALUE_HEADS, query_groups, HEAD_SIZE)
    deltas = lax.optimization_barrier(jnp.sum(output_gradient_wide * attention.astype(jnp.float32), axis=-1))
    normalized = weights / totals[..., None]
    dprobs = jnp.einsum('btkgd,bskd->bkgts', output_gradient_wide, values_win)
    dscores = return_journey(normalized * (dprobs - jnp.transpose(deltas, (0, 2, 3, 1))[..., None]))
    dq_hat = jnp.einsum('bkgts,bskd->btkgd', dscores, key_matrix) * inverse
    dk_win = jnp.einsum('bkgts,btkgd->bskd', dscores, query_matrix) * inverse
    dv_win = jnp.einsum('bkgts,btkgd->bskd', return_journey(normalized), output_gradient_wide)
    dk_total = fold_back(dk_win)
    value_gradient_total = fold_back(dv_win)
    query_raw_gradient, q_gain_part = q_back(dq_hat.reshape(sequence_length, QUERY_HEADS, HEAD_SIZE))
    key_raw_gradient, k_gain_part = k_back(dk_total)
    packed_row_gradient = jnp.concatenate([query_raw_gradient.reshape(sequence_length, QUERY_HEADS * HEAD_SIZE), key_raw_gradient.reshape(sequence_length, KEY_VALUE_HEADS * HEAD_SIZE), value_gradient_total.reshape(sequence_length, KEY_VALUE_HEADS * HEAD_SIZE)], axis=1).astype(jnp.bfloat16)
    return (attention.reshape(sequence_length, QUERY_HEADS * HEAD_SIZE), packed_row_gradient, q_gain_part, k_gain_part)

def reference(rollout_rows, dest_rank, doc_ids, advantage, out_grad, q_gain, k_gain):
    sequence_length = rollout_rows.shape[1]
    positions = jnp.broadcast_to(jnp.arange(sequence_length, dtype=jnp.int32)[None, :], dest_rank.shape)
    packed_input = jnp.zeros_like(rollout_rows).at[dest_rank, positions].set(rollout_rows)

    def one_pack(pack_items):
        return pack_window(pack_items[0], pack_items[1], pack_items[2], pack_items[3], q_gain, k_gain)
    attn_out, packed_row_gradient, q_parts, k_parts = lax.map(one_pack, (packed_input, doc_ids, advantage, out_grad))
    return (attn_out, packed_row_gradient, lax.optimization_barrier(jnp.sum(q_parts, axis=0)), lax.optimization_barrier(jnp.sum(k_parts, axis=0)))
```

```python
import functools
import math

import jax
import jax.numpy as jnp
from jax import lax
from jax.experimental import pallas as pl
from jax.experimental.pallas import tpu as pltpu
from jax.sharding import PartitionSpec as P

QUERY_HEADS = 32
KEY_VALUE_HEADS = 4
HEAD_SIZE = 128
GROUP = QUERY_HEADS // KEY_VALUE_HEADS
GROUP_WIDTH = GROUP * HEAD_SIZE
QUERY_WIDTH = QUERY_HEADS * HEAD_SIZE
KEY_WIDTH = KEY_VALUE_HEADS * HEAD_SIZE
CHUNKS = KEY_VALUE_HEADS + 1

epsilon = 1e-06
f32 = jnp.float32
bf16 = jnp.bfloat16
MESH = pl.DeviceIdType.MESH
LAST = (((1,), (1,)), ((), ()))


def matmul(a, b):
    return jnp.dot(a, b, preferred_element_type=f32)


def matmul_last(a, b):
    return lax.dot_general(a, b, LAST, preferred_element_type=f32)


def kernel(
    n_ranks, n_blocks, reach, capacity, pitch,
    rows_ref, dest_ref, docs_ref, adv_ref, grad_ref, q_gain_ref, k_gain_ref,
    attn_ref, out_ref, q_sum_ref, k_sum_ref,
    dest_all, docs_all, send, recv, place, kv_raw, kv_win, allowed,
    prob_s, dscore_s, q_s, d_s, part, ret, gain_ctx, gain_dp,
    dest_send, dest_recv, docs_send, docs_recv, row_send, row_recv,
    kv_send, kv_recv, ret_send, ret_recv, gc_send, gc_recv, gd_send, gd_recv,
):
    tokens = rows_ref.shape[1]
    keys = (reach + 1) * tokens
    me = lax.axis_index("dp")
    block = lax.axis_index("ctx")
    inverse = HEAD_SIZE ** (-0.5)

    barrier = pltpu.get_barrier_semaphore()

    def greet_dp(o, _):
        pl.semaphore_signal(
            barrier, inc=1, device_id={"dp": lax.rem(me + o, n_ranks)}, device_id_type=MESH
        )
        return 0

    def greet_ctx(o, _):
        pl.semaphore_signal(
            barrier, inc=1, device_id={"ctx": lax.rem(block + o, n_blocks)}, device_id_type=MESH
        )
        return 0

    lax.fori_loop(1, n_ranks, greet_dp, 0)
    lax.fori_loop(1, n_blocks, greet_ctx, 0)

    dest_all[me] = dest_ref[...]
    docs_all[0] = docs_ref[...]
    gain_ctx[block] = jnp.zeros((8, HEAD_SIZE), f32)
    for c in range(CHUNKS):
        recv[c, pl.ds(pl.multiple_of(me * pitch, 16), pitch), :] = jnp.zeros(
            (pitch, GROUP_WIDTH), bf16
        )
    for d in range(1, reach + 1):

        @pl.when(block < d)
        def _():
            docs_all[d] = jnp.full((1, tokens), -1, jnp.int32)
            kv_win[:, d * tokens : (d + 1) * tokens, :] = jnp.zeros(
                (KEY_VALUE_HEADS, tokens, 2 * HEAD_SIZE), bf16
            )

        @pl.when(block + d >= n_blocks)
        def _():
            ret[d - 1] = jnp.zeros((KEY_VALUE_HEADS, tokens, 2 * HEAD_SIZE), bf16)

    slots = n_ranks * pitch
    slot_row = lax.broadcasted_iota(jnp.int32, (slots, tokens), 0)
    slot_rank = slot_row // pitch
    slot_place = (slot_row % pitch).astype(f32)
    earlier = (
        lax.broadcasted_iota(jnp.int32, (tokens, tokens), 0)
        <= lax.broadcasted_iota(jnp.int32, (tokens, tokens), 1)
    ).astype(f32).astype(bf16)
    diagonal = lax.broadcasted_iota(jnp.int32, (tokens, tokens), 0) == lax.broadcasted_iota(
        jnp.int32, (tokens, tokens), 1
    )

    def slot_table(hit):
        hits = jnp.where(hit, 1.0, 0.0)
        count = matmul(hits.astype(bf16), earlier)
        return jnp.where(count - 1.0 == slot_place, hits, 0.0)

    def column(row):
        return jnp.sum(jnp.where(diagonal, row.astype(f32), 0.0), axis=1, keepdims=True)

    going = slot_table((dest_ref[...] == slot_rank) & (slot_rank != me)).astype(bf16)

    pl.semaphore_wait(barrier, n_ranks - 1 + n_blocks - 1)

    def dest_copy(src, dst, to):
        return pltpu.make_async_remote_copy(
            src_ref=dest_all.at[src],
            dst_ref=dest_all.at[src],
            send_sem=dest_send.at[dst],
            recv_sem=dest_recv.at[src],
            device_id={"dp": to},
            device_id_type=MESH,
        )

    def row_copy(c, slot, home, to):
        return pltpu.make_async_remote_copy(
            src_ref=send.at[c, pl.ds(pl.multiple_of(slot * pitch, 16), pitch), :],
            dst_ref=recv.at[c, pl.ds(pl.multiple_of(home * pitch, 16), pitch), :],
            send_sem=row_send.at[c, slot],
            recv_sem=row_recv.at[c, home],
            device_id={"dp": to},
            device_id_type=MESH,
        )

    def docs_copy(d, to):
        return pltpu.make_async_remote_copy(
            src_ref=docs_all.at[0],
            dst_ref=docs_all.at[d],
            send_sem=docs_send.at[d - 1],
            recv_sem=docs_recv.at[d - 1],
            device_id={"ctx": to},
            device_id_type=MESH,
        )

    def kv_copy(d, to):
        return pltpu.make_async_remote_copy(
            src_ref=kv_win.at[:, pl.ds(0, tokens), :],
            dst_ref=kv_win.at[:, pl.ds(d * tokens, tokens), :],
            send_sem=kv_send.at[d - 1],
            recv_sem=kv_recv.at[d - 1],
            device_id={"ctx": to},
            device_id_type=MESH,
        )

    def ret_copy(d, g, to):
        return pltpu.make_async_remote_copy(
            src_ref=part.at[g, pl.ds(d * tokens, tokens), :],
            dst_ref=ret.at[d - 1, g],
            send_sem=ret_send.at[d - 1, g],
            recv_sem=ret_recv.at[d - 1, g],
            device_id={"ctx": to},
            device_id_type=MESH,
        )

    def loop(stop, body):
        def step(o, _):
            body(o)
            return 0

        lax.fori_loop(1, stop, step, 0)

    def ahead(o):
        return lax.rem(me + o, n_ranks)

    loop(n_ranks, lambda o: dest_copy(me, ahead(o), ahead(o)).start())
    for d in range(1, reach + 1):

        @pl.when(block + d < n_blocks)
        def _():
            docs_copy(d, block + d).start()

    for c in range(CHUNKS):
        first = QUERY_WIDTH if c == 0 else (c - 1) * GROUP_WIDTH
        send[c] = matmul(going, rows_ref[0, :, first : first + GROUP_WIDTH]).astype(bf16)
        loop(n_ranks, lambda o: row_copy(c, ahead(o), me, ahead(o)).start())

    loop(n_ranks, lambda o: dest_copy(ahead(o), me, ahead(o)).wait_recv())
    source = jnp.broadcast_to(dest_all[...], (n_ranks, pitch, tokens)).reshape(slots, tokens)
    coming = slot_table((source == me) & (slot_rank != me))
    place[...] = jnp.transpose(coming).astype(bf16)
    staying = column(jnp.where(dest_ref[...] == me, 1.0, 0.0))
    doc_column = column(docs_ref[...])
    advantage = jnp.zeros((tokens, 1), f32)
    for doc in range(adv_ref.shape[1]):
        advantage = advantage + jnp.where(
            doc_column == float(doc), adv_ref[0:1, doc : doc + 1], 0.0
        )

    def packed(c, first):
        loop(n_ranks, lambda o: row_copy(c, me, ahead(o), ahead(o)).wait_recv())
        local = rows_ref[0, :, pl.ds(first, GROUP_WIDTH)].astype(f32)
        return matmul(place[...], recv[c]) + local * staying

    def unit(values):
        scale = lax.rsqrt(jnp.mean(values * values, axis=-1, keepdims=True) + epsilon)
        return values * scale, scale

    kv = packed(0, QUERY_WIDTH)
    kv_raw[...] = kv
    for g in range(KEY_VALUE_HEADS):
        k_unit, _ = unit(kv[:, g * HEAD_SIZE : (g + 1) * HEAD_SIZE])
        kv_win[g, 0:tokens, 0:HEAD_SIZE] = (k_unit * k_gain_ref[...]).astype(bf16)
        kv_win[g, 0:tokens, HEAD_SIZE : 2 * HEAD_SIZE] = kv[
            :, KEY_WIDTH + g * HEAD_SIZE : KEY_WIDTH + (g + 1) * HEAD_SIZE
        ].astype(bf16)
    for d in range(1, reach + 1):

        @pl.when(block + d < n_blocks)
        def _():
            kv_copy(d, block + d).start()

    for d in range(1, reach + 1):

        @pl.when(block >= d)
        def _():
            docs_copy(d, block - d).wait_recv()

    my_docs = docs_ref[...].astype(f32)
    for d in range(reach + 1):
        same = column(docs_all[d]) == my_docs
        if d == 0:
            same = same & (
                lax.broadcasted_iota(jnp.int32, (tokens, tokens), 0)
                <= lax.broadcasted_iota(jnp.int32, (tokens, tokens), 1)
            )
        same = jnp.where(same, 1.0, 0.0)
        allowed[d * tokens : (d + 1) * tokens, 0:tokens] = same
        allowed[d * tokens : (d + 1) * tokens, tokens : 2 * tokens] = same

    for d in range(1, reach + 1):

        @pl.when(block >= d)
        def _():
            kv_copy(d, block - d).wait_recv()

    def one_group(g, q_gain_sum):
        first = pl.multiple_of(g * GROUP_WIDTH, GROUP_WIDTH)
        raw = packed(g + 1, first)
        grads = (
            grad_ref[0, :, pl.ds(first, GROUP_WIDTH)].astype(f32) * advantage
        ).astype(bf16)
        k = kv_win[g, :, 0:HEAD_SIZE]
        v = kv_win[g, :, HEAD_SIZE : 2 * HEAD_SIZE]
        k_across = jnp.transpose(k.astype(f32)).astype(bf16)
        v_across = jnp.transpose(v.astype(f32)).astype(bf16)
        for pair in range(GROUP // 2):
            a = slice(2 * pair * HEAD_SIZE, (2 * pair + 1) * HEAD_SIZE)
            b = slice((2 * pair + 1) * HEAD_SIZE, (2 * pair + 2) * HEAD_SIZE)
            across = slice(pair * 2 * tokens, (pair + 1) * 2 * tokens)
            q_unit, q_scale = unit(jnp.concatenate([raw[:, a], raw[:, b]], axis=0))
            q_hat = (q_unit * q_gain_ref[...]).astype(bf16)
            d_out = jnp.concatenate([grads[:, a], grads[:, b]], axis=0)
            score = matmul_last(k, q_hat)
            weight = jnp.exp2(score * (inverse * math.log2(math.e))) * allowed[...]
            total = jnp.sum(weight, axis=0, keepdims=True)
            share = 1.0 / total
            attn = (matmul(v_across, weight.astype(bf16)) * share).astype(bf16).astype(f32)
            delta = jnp.sum(jnp.transpose(d_out.astype(f32)) * attn, axis=0, keepdims=True)
            attn_rows = jnp.transpose(attn).astype(bf16)
            prob = weight * share
            dscore = (prob * (matmul_last(v, d_out) - delta)).astype(bf16)
            prob_s[:, across] = prob.astype(bf16)
            dscore_s[:, across] = dscore
            q_s[across, :] = q_hat
            d_s[across, :] = d_out
            dq_hat = jnp.transpose(matmul(k_across, dscore)) * inverse
            q_gain_sum = q_gain_sum + jnp.sum(dq_hat * q_unit, axis=0, keepdims=True)
            scaled = dq_hat * q_gain_ref[...]
            dq = (
                q_scale * (scaled - q_unit * jnp.mean(scaled * q_unit, axis=-1, keepdims=True))
            ).astype(bf16)
            for half, where in ((0, a), (1, b)):
                cols = pl.ds(pl.multiple_of(first + where.start, HEAD_SIZE), HEAD_SIZE)
                attn_ref[0, :, cols] = attn_rows[half * tokens : (half + 1) * tokens]
                out_ref[0, :, cols] = dq[half * tokens : (half + 1) * tokens]
        part[g, :, 0:HEAD_SIZE] = (matmul(dscore_s[...], q_s[...]) * inverse).astype(bf16)
        part[g, :, HEAD_SIZE : 2 * HEAD_SIZE] = matmul(prob_s[...], d_s[...]).astype(bf16)
        for d in range(1, reach + 1):

            @pl.when(block >= d)
            def _():
                ret_copy(d, g, block - d).start()

        return q_gain_sum

    q_gain_sum = lax.fori_loop(0, KEY_VALUE_HEADS, one_group, jnp.zeros((1, HEAD_SIZE), f32))

    for d in range(1, reach + 1):

        @pl.when(block + d < n_blocks)
        def _():
            for g in range(KEY_VALUE_HEADS):
                ret_copy(d, g, block + d).wait_recv()

    k_gain_sum = jnp.zeros((1, HEAD_SIZE), f32)
    for g in range(KEY_VALUE_HEADS):
        both = part[g, 0:tokens, :].astype(f32)
        for d in range(1, reach + 1):
            both = both + ret[d - 1, g].astype(f32)
        dk_hat = both[:, 0:HEAD_SIZE]
        k_unit, k_scale = unit(kv_raw[:, g * HEAD_SIZE : (g + 1) * HEAD_SIZE])
        k_gain_sum = k_gain_sum + jnp.sum(dk_hat * k_unit, axis=0, keepdims=True)
        scaled = dk_hat * k_gain_ref[...]
        dk = k_scale * (scaled - k_unit * jnp.mean(scaled * k_unit, axis=-1, keepdims=True))
        at = QUERY_WIDTH + g * HEAD_SIZE
        out_ref[0, :, at : at + HEAD_SIZE] = dk.astype(bf16)
        at = at + KEY_WIDTH
        out_ref[0, :, at : at + HEAD_SIZE] = both[:, HEAD_SIZE:].astype(bf16)

    def gain_copy(buffer, send_sems, recv_sems, axis, home, to):
        return pltpu.make_async_remote_copy(
            src_ref=buffer.at[home],
            dst_ref=buffer.at[home],
            send_sem=send_sems.at[to],
            recv_sem=recv_sems.at[home],
            device_id={axis: to},
            device_id_type=MESH,
        )

    def exchange(buffer, send_sems, recv_sems, axis, mine, count):
        def other(o):
            return lax.rem(mine + o, count)

        loop(count, lambda o: gain_copy(buffer, send_sems, recv_sems, axis, mine, other(o)).start())

        def arrive(o):
            pltpu.make_async_remote_copy(
                src_ref=buffer.at[mine],
                dst_ref=buffer.at[other(o)],
                send_sem=send_sems.at[other(o)],
                recv_sem=recv_sems.at[other(o)],
                device_id={axis: other(o)},
                device_id_type=MESH,
            ).wait_recv()

        loop(count, arrive)
        total = buffer[0]
        for i in range(1, count):
            total = total + buffer[i]
        return total

    gain_ctx[block, 0:1, :] = q_gain_sum
    gain_ctx[block, 1:2, :] = k_gain_sum
    gain_dp[me] = exchange(gain_ctx, gc_send, gc_recv, "ctx", block, n_blocks)
    total = exchange(gain_dp, gd_send, gd_recv, "dp", me, n_ranks)
    q_sum_ref[...] = total[0:1, :]
    k_sum_ref[...] = total[1:2, :]

    def sent_dp(o):
        dest_copy(me, ahead(o), ahead(o)).wait_send()
        for c in range(CHUNKS):
            row_copy(c, ahead(o), me, ahead(o)).wait_send()
        gain_copy(gain_dp, gd_send, gd_recv, "dp", me, ahead(o)).wait_send()

    loop(n_ranks, sent_dp)
    loop(
        n_blocks,
        lambda o: gain_copy(
            gain_ctx, gc_send, gc_recv, "ctx", block, lax.rem(block + o, n_blocks)
        ).wait_send(),
    )
    for d in range(1, reach + 1):

        @pl.when(block + d < n_blocks)
        def _():
            docs_copy(d, block + d).wait_send()
            kv_copy(d, block + d).wait_send()

        @pl.when(block >= d)
        def _():
            for g in range(KEY_VALUE_HEADS):
                ret_copy(d, g, block - d).wait_send()


def per_device(n_ranks, n_blocks, rows, dest_rank, doc_ids, advantage, out_grad, q_gain, k_gain):
    tokens = rows.shape[1]
    width = rows.shape[2]
    reach = min(4, n_blocks - 1)
    capacity = tokens // n_ranks
    pitch = -(-capacity // 16) * 16
    slots = n_ranks * pitch
    keys = (reach + 1) * tokens
    stacked = GROUP * tokens
    vmem = pl.BlockSpec(memory_space=pltpu.VMEM)
    dma = pltpu.SemaphoreType.DMA
    attn, grads, q_sum, k_sum = pl.pallas_call(
        functools.partial(kernel, n_ranks, n_blocks, reach, capacity, pitch),
        out_shape=(
            jax.ShapeDtypeStruct((1, tokens, QUERY_WIDTH), bf16),
            jax.ShapeDtypeStruct((1, tokens, width), bf16),
            jax.ShapeDtypeStruct((1, HEAD_SIZE), f32),
            jax.ShapeDtypeStruct((1, HEAD_SIZE), f32),
        ),
        in_specs=[vmem] * 7,
        out_specs=(vmem,) * 4,
        scratch_shapes=[
            pltpu.VMEM((n_ranks, 1, tokens), jnp.int32),
            pltpu.VMEM((reach + 1, 1, tokens), jnp.int32),
            pltpu.VMEM((CHUNKS, slots, GROUP_WIDTH), bf16),
            pltpu.VMEM((CHUNKS, slots, GROUP_WIDTH), bf16),
            pltpu.VMEM((tokens, slots), bf16),
            pltpu.VMEM((tokens, GROUP_WIDTH), f32),
            pltpu.VMEM((KEY_VALUE_HEADS, keys, 2 * HEAD_SIZE), bf16),
            pltpu.VMEM((keys, 2 * tokens), f32),
            pltpu.VMEM((keys, stacked), bf16),
            pltpu.VMEM((keys, stacked), bf16),
            pltpu.VMEM((stacked, HEAD_SIZE), bf16),
            pltpu.VMEM((stacked, HEAD_SIZE), bf16),
            pltpu.VMEM((KEY_VALUE_HEADS, keys, 2 * HEAD_SIZE), bf16),
            pltpu.VMEM((reach, KEY_VALUE_HEADS, tokens, 2 * HEAD_SIZE), bf16),
            pltpu.VMEM((n_blocks, 8, HEAD_SIZE), f32),
            pltpu.VMEM((n_ranks, 8, HEAD_SIZE), f32),
            dma((n_ranks,)),
            dma((n_ranks,)),
            dma((reach,)),
            dma((reach,)),
            dma((CHUNKS, n_ranks)),
            dma((CHUNKS, n_ranks)),
            dma((reach,)),
            dma((reach,)),
            dma((reach, KEY_VALUE_HEADS)),
            dma((reach, KEY_VALUE_HEADS)),
            dma((n_blocks,)),
            dma((n_blocks,)),
            dma((n_ranks,)),
            dma((n_ranks,)),
        ],
        compiler_params=pltpu.CompilerParams(
            collective_id=0, has_side_effects=True, vmem_limit_bytes=48 * 1024 * 1024
        ),
        name="grpo_window",
    )(
        rows,
        dest_rank,
        doc_ids,
        advantage,
        out_grad,
        q_gain.reshape(1, HEAD_SIZE),
        k_gain.reshape(1, HEAD_SIZE),
    )
    return attn, grads, q_sum.reshape(HEAD_SIZE), k_sum.reshape(HEAD_SIZE)


def solution(mesh):
    placed = (
        P("dp", "ctx", None),
        P("dp", "ctx"),
        P("dp", "ctx"),
        P("dp", None),
        P("dp", "ctx", None),
        P(),
        P(),
    )
    return jax.shard_map(
        functools.partial(per_device, mesh.shape["dp"], mesh.shape["ctx"]),
        mesh=mesh,
        in_specs=placed,
        out_specs=(P("dp", "ctx", None), P("dp", "ctx", None), P(), P()),
        check_vma=False,
    )
```

```python
import functools
import math

import jax
import jax.numpy as jnp
from jax import lax
from jax.experimental import pallas as pl
from jax.experimental.pallas import tpu as pltpu
from jax.sharding import PartitionSpec as P

QUERY_HEADS = 32
KEY_VALUE_HEADS = 4
HEAD_SIZE = 128
GROUP = QUERY_HEADS // KEY_VALUE_HEADS
GROUP_WIDTH = GROUP * HEAD_SIZE
QUERY_WIDTH = QUERY_HEADS * HEAD_SIZE
KEY_WIDTH = KEY_VALUE_HEADS * HEAD_SIZE
HALF_WIDTH = GROUP_WIDTH // 2
CHUNKS = 2 * (KEY_VALUE_HEADS + 1)

epsilon = 1e-06
f32 = jnp.float32
bf16 = jnp.bfloat16
MESH = pl.DeviceIdType.MESH
LAST = (((1,), (1,)), ((), ()))


def matmul(a, b):
    return jnp.dot(a, b, preferred_element_type=f32)


def matmul_last(a, b):
    return lax.dot_general(a, b, LAST, preferred_element_type=f32)


def kernel(
    n_ranks, n_blocks, reach, capacity, pitch,
    rows_hbm, dest_hbm, docs_hbm, adv_hbm, grad_hbm, q_gain_hbm, k_gain_hbm,
    attn_hbm, out_hbm, gain_hbm,
    attn_ref, out_ref, gain_ref, out_sem, rows_ref, dest_ref, docs_ref, adv_ref, grad_ref, q_gain_ref, k_gain_ref, in_sem, rows_sem,
    dest_all, docs_all, send, recv, place, kv_win, allowed,
    prob_s, dscore_s, q_s, d_s, part, ret, gain_ctx, gain_dp, gain_all,
    dest_send, dest_recv, docs_send, docs_recv, row_send, row_recv,
    kv_send, kv_recv, ret_send, ret_recv, gc_send, gc_recv, gd_send, gd_recv, ga_send, ga_recv,
):
    tokens = rows_hbm.shape[1]
    me = lax.axis_index("dp")
    block = lax.axis_index("ctx")
    inverse = HEAD_SIZE ** (-0.5)

    barrier = pltpu.get_barrier_semaphore()

    def loop(stop, body):
        if stop <= 8:
            for o in range(stop - 1, 0, -1):
                body(o)
        else:
            lax.fori_loop(1, stop, lambda o, _: (body(stop - o), 0)[1], 0)

    def ahead(o):
        if n_ranks & (n_ranks - 1):
            return lax.rem(me + o, n_ranks)
        bit, other = 1, 0
        while bit < n_ranks:
            other = other + lax.rem(lax.div(me, bit) + lax.div(o, bit), 2) * bit
            bit = 2 * bit
        return other

    if n_ranks <= 8:
        partners = [None] + [ahead(o) for o in range(1, n_ranks)]
        ahead = partners.__getitem__

    def beside(o):
        return lax.rem(block + o, n_blocks)

    def greet(axis, other):
        pl.semaphore_signal(barrier, inc=1, device_id={axis: other}, device_id_type=MESH)

    everyone = n_ranks * n_blocks <= 64
    others = [(p, q) for p in range(n_ranks) for q in range(n_blocks)][1:] if everyone else []

    def device(p, q):
        to_dp = me if p == 0 else ahead(p)
        to_ctx = block if q == 0 else beside(q)
        return to_dp * n_blocks + to_ctx, {"dp": to_dp, "ctx": to_ctx}

    if everyone:
        for p, q in others:
            pl.semaphore_signal(
                barrier, inc=1, device_id=device(p, q)[1], device_id_type=MESH
            )
    else:
        loop(n_ranks, lambda o: greet("dp", ahead(o)))
        loop(n_blocks, lambda o: greet("ctx", beside(o)))

    def first_column(c):
        return QUERY_WIDTH + c * HALF_WIDTH if c < 2 else (c - 2) * HALF_WIDTH

    small = [
        pltpu.make_async_copy(src, dst, in_sem.at[i])
        for i, (src, dst) in enumerate(
            [
                (dest_hbm, dest_ref),
                (docs_hbm, docs_ref),
                (adv_hbm, adv_ref),
                (q_gain_hbm, q_gain_ref),
                (k_gain_hbm, k_gain_ref),
                (grad_hbm, grad_ref),
            ]
        )
    ]
    wide = [
        pltpu.make_async_copy(
            rows_hbm.at[0, :, pl.ds(first_column(c), HALF_WIDTH)], rows_ref.at[c], rows_sem.at[c]
        )
        for c in range(CHUNKS)
    ]
    small[0].start()
    small[1].start()
    for copy in wide:
        copy.start()
    for copy in small[2:]:
        copy.start()
    small[0].wait()
    small[1].wait()
    dest_all[me] = dest_ref[...]
    docs_all[0] = docs_ref[...]

    slots = n_ranks * pitch
    slot_row = lax.broadcasted_iota(jnp.int32, (slots, tokens), 0)
    slot_rank = slot_row // pitch
    slot_place = (slot_row % pitch).astype(f32)
    earlier = (
        lax.broadcasted_iota(jnp.int32, (tokens, tokens), 0)
        <= lax.broadcasted_iota(jnp.int32, (tokens, tokens), 1)
    ).astype(f32).astype(bf16)
    diagonal = lax.broadcasted_iota(jnp.int32, (tokens, tokens), 0) == lax.broadcasted_iota(
        jnp.int32, (tokens, tokens), 1
    )

    def slot_table(hit):
        hits = jnp.where(hit, 1.0, 0.0)
        count = matmul(hits.astype(bf16), earlier)
        return jnp.where(count - 1.0 == slot_place, hits, 0.0)

    def column(row):
        return jnp.sum(jnp.where(diagonal, row.astype(f32), 0.0), axis=1, keepdims=True)

    going = slot_table((dest_ref[...] == slot_rank) & (slot_rank != me)).astype(bf16)

    pl.semaphore_wait(barrier, len(others) if everyone else n_ranks - 1 + n_blocks - 1)

    def dest_copy(src, dst, to):
        return pltpu.make_async_remote_copy(
            src_ref=dest_all.at[src],
            dst_ref=dest_all.at[src],
            send_sem=dest_send.at[dst],
            recv_sem=dest_recv.at[src],
            device_id={"dp": to},
            device_id_type=MESH,
        )

    def row_copy(c, slot, home, to):
        return pltpu.make_async_remote_copy(
            src_ref=send.at[c, pl.ds(pl.multiple_of(slot * pitch, 16), pitch), :],
            dst_ref=recv.at[c, pl.ds(pl.multiple_of(home * pitch, 16), pitch), :],
            send_sem=row_send.at[c, slot],
            recv_sem=row_recv.at[c, home],
            device_id={"dp": to},
            device_id_type=MESH,
        )

    def docs_copy(d, to):
        return pltpu.make_async_remote_copy(
            src_ref=docs_all.at[0],
            dst_ref=docs_all.at[d],
            send_sem=docs_send.at[d - 1],
            recv_sem=docs_recv.at[d - 1],
            device_id={"ctx": to},
            device_id_type=MESH,
        )

    def kv_copy(d, to):
        return pltpu.make_async_remote_copy(
            src_ref=kv_win.at[:, pl.ds(0, tokens), :],
            dst_ref=kv_win.at[:, pl.ds(d * tokens, tokens), :],
            send_sem=kv_send.at[d - 1],
            recv_sem=kv_recv.at[d - 1],
            device_id={"ctx": to},
            device_id_type=MESH,
        )

    def ret_copy(d, g, to):
        return pltpu.make_async_remote_copy(
            src_ref=part.at[g, pl.ds(d * tokens, tokens), :],
            dst_ref=ret.at[d - 1, g],
            send_sem=ret_send.at[d - 1, g],
            recv_sem=ret_recv.at[d - 1, g],
            device_id={"ctx": to},
            device_id_type=MESH,
        )

    loop(n_ranks, lambda o: dest_copy(me, ahead(o), ahead(o)).start())
    for d in range(1, reach + 1):

        @pl.when(block + d < n_blocks)
        def _():
            docs_copy(d, block + d).start()

    for c in range(CHUNKS):
        wide[c].wait()
        send[c] = matmul(going, rows_ref[c]).astype(bf16)
        loop(n_ranks, lambda o: row_copy(c, ahead(o), me, ahead(o)).start())

    for copy in small[2:]:
        copy.wait()
    gain_ctx[block] = jnp.zeros((8, HEAD_SIZE), f32)
    gain_ref[...] = jnp.zeros((8, HEAD_SIZE), f32)
    for c in range(CHUNKS):
        recv[c, pl.ds(pl.multiple_of(me * pitch, 16), pitch), :] = jnp.zeros(
            (pitch, HALF_WIDTH), bf16
        )
    for d in range(1, reach + 1):

        @pl.when(block < d)
        def _():
            docs_all[d] = jnp.full((1, tokens), -1, jnp.int32)
            kv_win[:, d * tokens : (d + 1) * tokens, :] = jnp.zeros(
                (KEY_VALUE_HEADS, tokens, 2 * HEAD_SIZE), bf16
            )

        @pl.when(block + d >= n_blocks)
        def _():
            ret[d - 1] = jnp.zeros((KEY_VALUE_HEADS, tokens, 2 * HEAD_SIZE), bf16)

    loop(n_ranks, lambda o: dest_copy(ahead(o), me, ahead(o)).wait_recv())
    source = jnp.broadcast_to(dest_all[...], (n_ranks, pitch, tokens)).reshape(slots, tokens)
    coming = slot_table((source == me) & (slot_rank != me))
    place[...] = jnp.transpose(coming).astype(bf16)
    staying = column(jnp.where(dest_ref[...] == me, 1.0, 0.0))
    doc_column = column(docs_ref[...])
    advantage = jnp.zeros((tokens, 1), f32)
    for doc in range(adv_ref.shape[1]):
        advantage = advantage + jnp.where(
            doc_column == float(doc), adv_ref[0:1, doc : doc + 1], 0.0
        )

    def packed(c):
        loop(n_ranks, lambda o: row_copy(c, me, ahead(o), ahead(o)).wait_recv())
        return matmul(place[...], recv[c]) + rows_ref[c].astype(f32) * staying

    def unit(values):
        scale = lax.rsqrt(jnp.mean(values * values, axis=-1, keepdims=True) + epsilon)
        return values * scale, scale

    for half in range(2):
        raw = packed(half).astype(bf16)
        for g in range(KEY_VALUE_HEADS):
            kv_win[g, 0:tokens, half * HEAD_SIZE : (half + 1) * HEAD_SIZE] = raw[
                :, g * HEAD_SIZE : (g + 1) * HEAD_SIZE
            ]
    for d in range(1, reach + 1):

        @pl.when(block + d < n_blocks)
        def _():
            kv_copy(d, block + d).start()

    for d in range(1, reach + 1):

        @pl.when(block >= d)
        def _():
            docs_copy(d, block - d).wait_recv()

    my_docs = docs_ref[...].astype(f32)
    for d in range(reach + 1):
        same = column(docs_all[d]) == my_docs
        if d == 0:
            same = same & (
                lax.broadcasted_iota(jnp.int32, (tokens, tokens), 0)
                <= lax.broadcasted_iota(jnp.int32, (tokens, tokens), 1)
            )
        same = jnp.where(same, 1.0, 0.0)
        allowed[d * tokens : (d + 1) * tokens, 0:tokens] = same
        allowed[d * tokens : (d + 1) * tokens, tokens : 2 * tokens] = same

    for d in range(1, reach + 1):

        @pl.when(block >= d)
        def _():
            kv_copy(d, block - d).wait_recv()

    def group_columns(g):
        return pl.ds(pl.multiple_of(g * GROUP_WIDTH, GROUP_WIDTH), GROUP_WIDTH)

    def attn_out_copy(g):
        return pltpu.make_async_copy(
            attn_ref.at[:, :, group_columns(g)], attn_hbm.at[:, :, group_columns(g)], out_sem.at[0, g]
        )

    def query_out_copy(g):
        return pltpu.make_async_copy(
            out_ref.at[:, :, group_columns(g)], out_hbm.at[:, :, group_columns(g)], out_sem.at[1, g]
        )

    def give_back(g):
        for d in range(1, reach + 1):

            @pl.when(block >= d)
            def _():
                ret_copy(d, g, block - d).start()

    def one_group(g, sums):
        q_gain_sum, k_gain_sum = sums
        first = pl.multiple_of(g * GROUP_WIDTH, GROUP_WIDTH)
        k_unit, _ = unit(kv_win[g, :, 0:HEAD_SIZE].astype(f32))
        k = (k_unit * k_gain_ref[...]).astype(bf16)
        v = kv_win[g, :, HEAD_SIZE : 2 * HEAD_SIZE]
        k_across = jnp.transpose(k.astype(f32)).astype(bf16)
        v_across = jnp.transpose(v.astype(f32)).astype(bf16)
        for pair in range(GROUP // 2):
            if pair % (GROUP // 4) == 0:
                half = pair // (GROUP // 4)
                raw = packed(2 * g + 2 + half)
                base = pl.multiple_of(first + half * HALF_WIDTH, HALF_WIDTH)
                grads = (
                    grad_ref[0, :, pl.ds(base, HALF_WIDTH)].astype(f32) * advantage
                ).astype(bf16)
            at = pair % (GROUP // 4)
            a = slice(2 * at * HEAD_SIZE, (2 * at + 1) * HEAD_SIZE)
            b = slice((2 * at + 1) * HEAD_SIZE, (2 * at + 2) * HEAD_SIZE)
            across = slice(pair * 2 * tokens, (pair + 1) * 2 * tokens)
            q_unit, q_scale = unit(jnp.concatenate([raw[:, a], raw[:, b]], axis=0))
            q_hat = (q_unit * q_gain_ref[...]).astype(bf16)
            d_out = jnp.concatenate([grads[:, a], grads[:, b]], axis=0)
            score = matmul_last(k, q_hat)
            weight = jnp.exp2(score * (inverse * math.log2(math.e))) * allowed[...]
            total = jnp.sum(weight, axis=0, keepdims=True)
            share = 1.0 / total
            attn = (matmul(v_across, weight.astype(bf16)) * share).astype(bf16).astype(f32)
            delta = jnp.sum(jnp.transpose(d_out.astype(f32)) * attn, axis=0, keepdims=True)
            attn_rows = jnp.transpose(attn).astype(bf16)
            prob = weight * share
            dscore = (prob * (matmul_last(v, d_out) - delta)).astype(bf16)
            prob_s[:, across] = prob.astype(bf16)
            dscore_s[:, across] = dscore
            q_s[across, :] = q_hat
            d_s[across, :] = d_out
            dq_hat = jnp.transpose(matmul(k_across, dscore)) * inverse
            q_gain_sum = q_gain_sum + jnp.sum(dq_hat * q_unit, axis=0, keepdims=True)
            scaled = dq_hat * q_gain_ref[...]
            dq = (
                q_scale * (scaled - q_unit * jnp.mean(scaled * q_unit, axis=-1, keepdims=True))
            ).astype(bf16)
            for i, where in ((0, a), (1, b)):
                cols = pl.ds(pl.multiple_of(base + where.start, HEAD_SIZE), HEAD_SIZE)
                attn_ref[0, :, cols] = attn_rows[i * tokens : (i + 1) * tokens]
                out_ref[0, :, cols] = dq[i * tokens : (i + 1) * tokens]
        dk_part = (matmul(dscore_s[...], q_s[...]) * inverse).astype(bf16)
        part[g, :, 0:HEAD_SIZE] = dk_part
        part[g, :, HEAD_SIZE : 2 * HEAD_SIZE] = matmul(prob_s[...], d_s[...]).astype(bf16)
        @pl.when(g < KEY_VALUE_HEADS - 1)
        def _():
            give_back(g)

        attn_out_copy(g).start()
        query_out_copy(g).start()

        k_gain_sum = k_gain_sum + jnp.sum(dk_part.astype(f32) * k_unit, axis=0, keepdims=True)
        return q_gain_sum, k_gain_sum

    none = jnp.zeros((1, HEAD_SIZE), f32)
    q_gain_sum, k_gain_sum = lax.fori_loop(0, KEY_VALUE_HEADS, one_group, (none, none))

    def gain_copy(buffer, send_sems, recv_sems, axis, home, to, other):
        return pltpu.make_async_remote_copy(
            src_ref=buffer.at[home],
            dst_ref=buffer.at[to],
            send_sem=send_sems.at[other],
            recv_sem=recv_sems.at[to],
            device_id={axis: other},
            device_id_type=MESH,
        )

    over_ctx = functools.partial(gain_copy, gain_ctx, gc_send, gc_recv, "ctx", block)
    over_dp = functools.partial(gain_copy, gain_dp, gd_send, gd_recv, "dp", me)

    def summed(buffer, count):
        total = buffer[0]
        for i in range(1, count):
            total = total + buffer[i]
        return total

    def gain_to(p, q):
        home = me * n_blocks + block
        index, to = device(p, q)
        return pltpu.make_async_remote_copy(
            src_ref=gain_all.at[home],
            dst_ref=gain_all.at[home],
            send_sem=ga_send.at[index],
            recv_sem=ga_recv.at[home],
            device_id=to,
            device_id_type=MESH,
        )

    def gain_from(p, q):
        index, to = device(p, q)
        return pltpu.make_async_remote_copy(
            src_ref=gain_all.at[index],
            dst_ref=gain_all.at[index],
            send_sem=ga_send.at[index],
            recv_sem=ga_recv.at[index],
            device_id=to,
            device_id_type=MESH,
        )

    if everyone:
        gain_all[me * n_blocks + block, 0:1, :] = q_gain_sum
        gain_all[me * n_blocks + block, 1:2, :] = k_gain_sum
        for p, q in others:
            gain_to(p, q).start()
        give_back(KEY_VALUE_HEADS - 1)
    else:
        give_back(KEY_VALUE_HEADS - 1)
        gain_ctx[block, 0:1, :] = q_gain_sum
        gain_ctx[block, 1:2, :] = k_gain_sum
        loop(n_blocks, lambda o: over_ctx(block, beside(o)).start())
        loop(n_blocks, lambda o: over_ctx(beside(o), beside(o)).wait_recv())
        gain_dp[me] = summed(gain_ctx, n_blocks)
        loop(n_ranks, lambda o: over_dp(me, ahead(o)).start())

    for d in range(1, reach + 1):

        @pl.when(block + d < n_blocks)
        def _():
            for g in range(KEY_VALUE_HEADS):
                ret_copy(d, g, block + d).wait_recv()

    for g in range(KEY_VALUE_HEADS):
        both = part[g, 0:tokens, :].astype(f32)
        for d in range(1, reach + 1):
            both = both + ret[d - 1, g].astype(f32)
        k_unit, k_scale = unit(kv_win[g, 0:tokens, 0:HEAD_SIZE].astype(f32))
        scaled = both[:, 0:HEAD_SIZE] * k_gain_ref[...]
        dk = k_scale * (scaled - k_unit * jnp.mean(scaled * k_unit, axis=-1, keepdims=True))
        at = QUERY_WIDTH + g * HEAD_SIZE
        out_ref[0, :, at : at + HEAD_SIZE] = dk.astype(bf16)
        at = at + KEY_WIDTH
        out_ref[0, :, at : at + HEAD_SIZE] = both[:, HEAD_SIZE:].astype(bf16)

    last = pl.ds(QUERY_WIDTH, 2 * KEY_WIDTH)
    last_out = pltpu.make_async_copy(
        out_ref.at[:, :, last], out_hbm.at[:, :, last], out_sem.at[0, KEY_VALUE_HEADS]
    )
    last_out.start()
    if everyone:
        for p, q in others:
            gain_from(p, q).wait_recv()
        gain_ref[0:2, :] = jnp.sum(gain_all[...], axis=0)
    else:
        loop(n_ranks, lambda o: over_dp(ahead(o), ahead(o)).wait_recv())
        gain_ref[...] = summed(gain_dp, n_ranks)
    gain_out = pltpu.make_async_copy(gain_ref, gain_hbm, out_sem.at[1, KEY_VALUE_HEADS])
    gain_out.start()

    for g in range(KEY_VALUE_HEADS):
        attn_out_copy(g).wait()
        query_out_copy(g).wait()
    last_out.wait()
    gain_out.wait()
    def sent_dp(o):
        dest_copy(me, ahead(o), ahead(o)).wait_send()
        for c in range(CHUNKS):
            row_copy(c, ahead(o), me, ahead(o)).wait_send()
        if not everyone:
            over_dp(me, ahead(o)).wait_send()

    loop(n_ranks, sent_dp)
    for p, q in others:
        gain_to(p, q).wait_send()
    if not everyone:
        loop(n_blocks, lambda o: over_ctx(block, beside(o)).wait_send())
    for d in range(1, reach + 1):

        @pl.when(block + d < n_blocks)
        def _():
            docs_copy(d, block + d).wait_send()
            kv_copy(d, block + d).wait_send()

        @pl.when(block >= d)
        def _():
            for g in range(KEY_VALUE_HEADS):
                ret_copy(d, g, block - d).wait_send()


def write_out(attn_in, grads_in, gains, attn, grads, q_sum, k_sum, attn_v, grads_v, gains_v, in_sems, out_sems):
    ways = [(gains, gains_v, gains_v.at[pl.ds(0, 1), :], q_sum)]
    step = attn_in.shape[1] // 4
    for i in range(4):
        rows = (slice(None), pl.ds(i * step, step), slice(None))
        ways.append((attn_in.at[rows], attn_v.at[rows], attn_v.at[rows], attn.at[rows]))
        ways.append((grads_in.at[rows], grads_v.at[rows], grads_v.at[rows], grads.at[rows]))
    come = [pltpu.make_async_copy(w[0], w[1], in_sems.at[i]) for i, w in enumerate(ways)]
    go = [pltpu.make_async_copy(w[2], w[3], out_sems.at[i]) for i, w in enumerate(ways)]
    second = pltpu.make_async_copy(gains_v.at[pl.ds(1, 1), :], k_sum, out_sems.at[len(ways)])
    for copy in come:
        copy.start()
    for i in range(len(ways)):
        come[i].wait()
        go[i].start()
        if i == 0:
            second.start()
    for copy in go:
        copy.wait()
    second.wait()


def per_device(n_ranks, n_blocks, rows, dest_rank, doc_ids, advantage, out_grad, q_gain, k_gain):
    tokens = rows.shape[1]
    width = rows.shape[2]
    reach = min(4, n_blocks - 1)
    capacity = tokens // n_ranks
    pitch = -(-capacity // 16) * 16
    slots = n_ranks * pitch
    keys = (reach + 1) * tokens
    stacked = GROUP * tokens
    direct = n_ranks * n_blocks if n_ranks * n_blocks <= 64 else 1
    dma = pltpu.SemaphoreType.DMA
    hbm = pl.BlockSpec(memory_space=pltpu.HBM)
    results = (
        jax.ShapeDtypeStruct((1, tokens, QUERY_WIDTH), bf16),
        jax.ShapeDtypeStruct((1, tokens, width), bf16),
        jax.ShapeDtypeStruct((1, HEAD_SIZE), f32),
        jax.ShapeDtypeStruct((1, HEAD_SIZE), f32),
    )
    partial = pl.pallas_call(
        functools.partial(kernel, n_ranks, n_blocks, reach, capacity, pitch),
        out_shape=(*results[:2], jax.ShapeDtypeStruct((8, HEAD_SIZE), f32)),
        in_specs=[hbm] * 7,
        out_specs=(hbm,) * 3,
        scratch_shapes=[
            pltpu.VMEM((1, tokens, QUERY_WIDTH), bf16),
            pltpu.VMEM((1, tokens, width), bf16),
            pltpu.VMEM((8, HEAD_SIZE), f32),
            dma((2, KEY_VALUE_HEADS + 1)),
            pltpu.VMEM((CHUNKS, tokens, HALF_WIDTH), bf16),
            pltpu.VMEM((1, tokens), jnp.int32),
            pltpu.VMEM((1, tokens), jnp.int32),
            pltpu.VMEM(advantage.shape, f32),
            pltpu.VMEM((1, tokens, QUERY_WIDTH), bf16),
            pltpu.VMEM((1, HEAD_SIZE), f32),
            pltpu.VMEM((1, HEAD_SIZE), f32),
            dma((6,)),
            dma((CHUNKS,)),
            pltpu.VMEM((n_ranks, 1, tokens), jnp.int32),
            pltpu.VMEM((reach + 1, 1, tokens), jnp.int32),
            pltpu.VMEM((CHUNKS, slots, HALF_WIDTH), bf16),
            pltpu.VMEM((CHUNKS, slots, HALF_WIDTH), bf16),
            pltpu.VMEM((tokens, slots), bf16),
            pltpu.VMEM((KEY_VALUE_HEADS, keys, 2 * HEAD_SIZE), bf16),
            pltpu.VMEM((keys, 2 * tokens), f32),
            pltpu.VMEM((keys, stacked), bf16),
            pltpu.VMEM((keys, stacked), bf16),
            pltpu.VMEM((stacked, HEAD_SIZE), bf16),
            pltpu.VMEM((stacked, HEAD_SIZE), bf16),
            pltpu.VMEM((KEY_VALUE_HEADS, keys, 2 * HEAD_SIZE), bf16),
            pltpu.VMEM((reach, KEY_VALUE_HEADS, tokens, 2 * HEAD_SIZE), bf16),
            pltpu.VMEM((n_blocks, 8, HEAD_SIZE), f32),
            pltpu.VMEM((n_ranks, 8, HEAD_SIZE), f32),
            pltpu.VMEM((direct, 2, HEAD_SIZE), f32),
            dma((n_ranks,)),
            dma((n_ranks,)),
            dma((reach,)),
            dma((reach,)),
            dma((CHUNKS, n_ranks)),
            dma((CHUNKS, n_ranks)),
            dma((reach,)),
            dma((reach,)),
            dma((reach, KEY_VALUE_HEADS)),
            dma((reach, KEY_VALUE_HEADS)),
            dma((n_blocks,)),
            dma((n_blocks,)),
            dma((n_ranks,)),
            dma((n_ranks,)),
            dma((direct,)),
            dma((direct,)),
        ],
        compiler_params=pltpu.CompilerParams(
            collective_id=0, has_side_effects=True, vmem_limit_bytes=62 * 1024 * 1024
        ),
        name="grpo_window",
    )(
        rows,
        dest_rank,
        doc_ids,
        advantage,
        out_grad,
        q_gain.reshape(1, HEAD_SIZE),
        k_gain.reshape(1, HEAD_SIZE),
    )
    attn, grads, q_sum, k_sum = pl.pallas_call(
        write_out,
        out_shape=results,
        in_specs=[hbm] * 3,
        out_specs=(hbm,) * 4,
        scratch_shapes=[
            pltpu.VMEM((1, tokens, QUERY_WIDTH), bf16),
            pltpu.VMEM((1, tokens, width), bf16),
            pltpu.VMEM(partial[2].shape, f32),
            dma((9,)),
            dma((10,)),
        ],
        compiler_params=pltpu.CompilerParams(vmem_limit_bytes=62 * 1024 * 1024),
        name="write_out",
    )(*partial)
    return attn, grads, q_sum.reshape(HEAD_SIZE), k_sum.reshape(HEAD_SIZE)


def solution(mesh):
    placed = (
        P("dp", "ctx", None),
        P("dp", "ctx"),
        P("dp", "ctx"),
        P("dp", None),
        P("dp", "ctx", None),
        P(),
        P(),
    )
    return jax.shard_map(
        functools.partial(per_device, mesh.shape["dp"], mesh.shape["ctx"]),
        mesh=mesh,
        in_specs=placed,
        out_specs=(P("dp", "ctx", None), P("dp", "ctx", None), P(), P()),
        check_vma=False,
    )
```

```python
import functools
import math

import jax
import jax.numpy as jnp
from jax import lax
from jax.experimental import pallas as pl
from jax.experimental.pallas import tpu as pltpu
from jax.sharding import PartitionSpec as P

QUERY_HEADS = 32
KEY_VALUE_HEADS = 4
HEAD_SIZE = 128
GROUP = QUERY_HEADS // KEY_VALUE_HEADS
GROUP_WIDTH = GROUP * HEAD_SIZE
QUERY_WIDTH = QUERY_HEADS * HEAD_SIZE
KEY_WIDTH = KEY_VALUE_HEADS * HEAD_SIZE
HALF_WIDTH = GROUP_WIDTH // 2
CHUNKS = 2 * (KEY_VALUE_HEADS + 1)

epsilon = 1e-06
f32 = jnp.float32
bf16 = jnp.bfloat16
MESH = pl.DeviceIdType.MESH
LAST = (((1,), (1,)), ((), ()))


def matmul(a, b):
    return jnp.dot(a, b, preferred_element_type=f32)


def matmul_last(a, b):
    return lax.dot_general(a, b, LAST, preferred_element_type=f32)


def kernel(
    n_ranks, n_blocks, reach, capacity, pitch,
    rows_hbm, dest_hbm, docs_hbm, adv_hbm, grad_hbm, q_gain_hbm, k_gain_hbm,
    attn_hbm, out_hbm, gain_hbm,
    attn_ref, out_ref, gain_ref, out_sem, rows_ref, dest_ref, docs_ref, adv_ref, grad_ref, q_gain_ref, k_gain_ref, in_sem, rows_sem,
    dest_all, docs_all, send, recv, place, kv_win, allowed,
    prob_s, dscore_s, q_s, d_s, part, ret, gain_ctx, gain_dp, gain_all,
    dest_send, dest_recv, docs_send, docs_recv, row_send, row_recv,
    kv_send, kv_recv, ret_send, ret_recv, gc_send, gc_recv, gd_send, gd_recv, ga_send, ga_recv,
):
    tokens = rows_hbm.shape[1]
    me = lax.axis_index("dp")
    block = lax.axis_index("ctx")
    inverse = HEAD_SIZE ** (-0.5)

    barrier = pltpu.get_barrier_semaphore()

    def loop(stop, body):
        if stop <= 8:
            for o in range(1, stop):
                body(o)
        else:
            lax.fori_loop(1, stop, lambda o, _: (body(stop - o), 0)[1], 0)

    def ahead(o):
        if n_ranks & (n_ranks - 1):
            return lax.rem(me + o, n_ranks)
        bit, other = 1, 0
        while bit < n_ranks:
            other = other + lax.rem(lax.div(me, bit) + lax.div(o, bit), 2) * bit
            bit = 2 * bit
        return other

    if n_ranks <= 8:
        partners = [None] + [ahead(o) for o in range(1, n_ranks)]
        ahead = partners.__getitem__

    def beside(o):
        return lax.rem(block + o, n_blocks)

    def greet(axis, other):
        pl.semaphore_signal(barrier, inc=1, device_id={axis: other}, device_id_type=MESH)

    def first_column(c):
        return QUERY_WIDTH + c * HALF_WIDTH if c < 2 else (c - 2) * HALF_WIDTH

    small = [
        pltpu.make_async_copy(src, dst, in_sem.at[i])
        for i, (src, dst) in enumerate(
            [
                (dest_hbm, dest_ref),
                (docs_hbm, docs_ref),
                (adv_hbm, adv_ref),
                (q_gain_hbm, q_gain_ref),
                (k_gain_hbm, k_gain_ref),
                (grad_hbm, grad_ref),
            ]
        )
    ]
    wide = [
        pltpu.make_async_copy(
            rows_hbm.at[0, :, pl.ds(first_column(c), HALF_WIDTH)], rows_ref.at[c], rows_sem.at[c]
        )
        for c in range(CHUNKS)
    ]
    small[0].start()
    wide[0].start()

    everyone = n_ranks * n_blocks <= 64
    others = [(p, q) for p in range(n_ranks) for q in range(n_blocks)][1:] if everyone else []

    def device(p, q):
        to_dp = me if p == 0 else ahead(p)
        to_ctx = block if q == 0 else beside(q)
        return to_dp * n_blocks + to_ctx, {"dp": to_dp, "ctx": to_ctx}

    if everyone:
        for p, q in others:
            pl.semaphore_signal(
                barrier, inc=1, device_id=device(p, q)[1], device_id_type=MESH
            )
    else:
        loop(n_ranks, lambda o: greet("dp", ahead(o)))
        loop(n_blocks, lambda o: greet("ctx", beside(o)))

    small[1].start()
    for copy in wide[1:]:
        copy.start()
    for copy in small[2:]:
        copy.start()
    small[0].wait()
    small[1].wait()
    dest_all[me] = dest_ref[...]
    docs_all[0] = docs_ref[...]

    slots = n_ranks * pitch
    slot_row = lax.broadcasted_iota(jnp.int32, (slots, tokens), 0)
    slot_rank = slot_row // pitch
    slot_place = (slot_row % pitch).astype(f32)
    earlier = (
        lax.broadcasted_iota(jnp.int32, (tokens, tokens), 0)
        <= lax.broadcasted_iota(jnp.int32, (tokens, tokens), 1)
    ).astype(f32).astype(bf16)
    diagonal = lax.broadcasted_iota(jnp.int32, (tokens, tokens), 0) == lax.broadcasted_iota(
        jnp.int32, (tokens, tokens), 1
    )

    def slot_table(hit):
        hits = jnp.where(hit, 1.0, 0.0)
        count = matmul(hits.astype(bf16), earlier)
        return jnp.where(count - 1.0 == slot_place, hits, 0.0)

    def column(row):
        return jnp.sum(jnp.where(diagonal, row.astype(f32), 0.0), axis=1, keepdims=True)

    going = slot_table((dest_ref[...] == slot_rank) & (slot_rank != me)).astype(bf16)

    pl.semaphore_wait(barrier, len(others) if everyone else n_ranks - 1 + n_blocks - 1)

    def dest_copy(src, dst, to):
        return pltpu.make_async_remote_copy(
            src_ref=dest_all.at[src],
            dst_ref=dest_all.at[src],
            send_sem=dest_send.at[dst],
            recv_sem=dest_recv.at[src],
            device_id={"dp": to},
            device_id_type=MESH,
        )

    def row_copy(c, slot, home, to):
        return pltpu.make_async_remote_copy(
            src_ref=send.at[c, pl.ds(pl.multiple_of(slot * pitch, 16), pitch), :],
            dst_ref=recv.at[c, pl.ds(pl.multiple_of(home * pitch, 16), pitch), :],
            send_sem=row_send.at[c, slot],
            recv_sem=row_recv.at[c, home],
            device_id={"dp": to},
            device_id_type=MESH,
        )

    def docs_copy(d, to):
        return pltpu.make_async_remote_copy(
            src_ref=docs_all.at[0],
            dst_ref=docs_all.at[d],
            send_sem=docs_send.at[d - 1],
            recv_sem=docs_recv.at[d - 1],
            device_id={"ctx": to},
            device_id_type=MESH,
        )

    def kv_copy(d, to):
        return pltpu.make_async_remote_copy(
            src_ref=kv_win.at[:, pl.ds(0, tokens), :],
            dst_ref=kv_win.at[:, pl.ds(d * tokens, tokens), :],
            send_sem=kv_send.at[d - 1],
            recv_sem=kv_recv.at[d - 1],
            device_id={"ctx": to},
            device_id_type=MESH,
        )

    def ret_copy(d, g, to):
        return pltpu.make_async_remote_copy(
            src_ref=part.at[g, pl.ds(d * tokens, tokens), :],
            dst_ref=ret.at[d - 1, g],
            send_sem=ret_send.at[d - 1, g],
            recv_sem=ret_recv.at[d - 1, g],
            device_id={"ctx": to},
            device_id_type=MESH,
        )

    loop(n_ranks, lambda o: dest_copy(me, ahead(o), ahead(o)).start())
    for d in range(1, reach + 1):

        @pl.when(block + d < n_blocks)
        def _():
            docs_copy(d, block + d).start()

    for c in range(CHUNKS):
        wide[c].wait()
        send[c] = matmul(going, rows_ref[c]).astype(bf16)
        loop(n_ranks, lambda o: row_copy(c, ahead(o), me, ahead(o)).start())

    for copy in small[2:]:
        copy.wait()
    gain_ctx[block] = jnp.zeros((8, HEAD_SIZE), f32)
    gain_ref[...] = jnp.zeros((8, HEAD_SIZE), f32)
    for c in range(CHUNKS):
        recv[c, pl.ds(pl.multiple_of(me * pitch, 16), pitch), :] = jnp.zeros(
            (pitch, HALF_WIDTH), bf16
        )
    for d in range(1, reach + 1):

        @pl.when(block < d)
        def _():
            docs_all[d] = jnp.full((1, tokens), -1, jnp.int32)
            kv_win[:, d * tokens : (d + 1) * tokens, :] = jnp.zeros(
                (KEY_VALUE_HEADS, tokens, 2 * HEAD_SIZE), bf16
            )

        @pl.when(block + d >= n_blocks)
        def _():
            ret[d - 1] = jnp.zeros((KEY_VALUE_HEADS, tokens, 2 * HEAD_SIZE), bf16)

    loop(n_ranks, lambda o: dest_copy(ahead(o), me, ahead(o)).wait_recv())
    source = jnp.broadcast_to(dest_all[...], (n_ranks, pitch, tokens)).reshape(slots, tokens)
    coming = slot_table((source == me) & (slot_rank != me))
    place[...] = jnp.transpose(coming).astype(bf16)
    staying = column(jnp.where(dest_ref[...] == me, 1.0, 0.0))
    doc_column = column(docs_ref[...])
    advantage = jnp.zeros((tokens, 1), f32)
    for doc in range(adv_ref.shape[1]):
        advantage = advantage + jnp.where(
            doc_column == float(doc), adv_ref[0:1, doc : doc + 1], 0.0
        )

    def packed(c):
        loop(n_ranks, lambda o: row_copy(c, me, ahead(o), ahead(o)).wait_recv())
        return matmul(place[...], recv[c]) + rows_ref[c].astype(f32) * staying

    def unit(values):
        scale = lax.rsqrt(jnp.mean(values * values, axis=-1, keepdims=True) + epsilon)
        return values * scale, scale

    for half in range(2):
        raw = packed(half).astype(bf16)
        for g in range(KEY_VALUE_HEADS):
            kv_win[g, 0:tokens, half * HEAD_SIZE : (half + 1) * HEAD_SIZE] = raw[
                :, g * HEAD_SIZE : (g + 1) * HEAD_SIZE
            ]
    for d in range(1, reach + 1):

        @pl.when(block + d < n_blocks)
        def _():
            kv_copy(d, block + d).start()

    for d in range(1, reach + 1):

        @pl.when(block >= d)
        def _():
            docs_copy(d, block - d).wait_recv()

    my_docs = docs_ref[...].astype(f32)
    for d in range(reach + 1):
        same = column(docs_all[d]) == my_docs
        if d == 0:
            same = same & (
                lax.broadcasted_iota(jnp.int32, (tokens, tokens), 0)
                <= lax.broadcasted_iota(jnp.int32, (tokens, tokens), 1)
            )
        same = jnp.where(same, 1.0, 0.0)
        allowed[d * tokens : (d + 1) * tokens, 0:tokens] = same
        allowed[d * tokens : (d + 1) * tokens, tokens : 2 * tokens] = same

    for d in range(1, reach + 1):

        @pl.when(block >= d)
        def _():
            kv_copy(d, block - d).wait_recv()

    def group_columns(g):
        return pl.ds(pl.multiple_of(g * GROUP_WIDTH, GROUP_WIDTH), GROUP_WIDTH)

    def attn_out_copy(g):
        return pltpu.make_async_copy(
            attn_ref.at[:, :, group_columns(g)], attn_hbm.at[:, :, group_columns(g)], out_sem.at[0, g]
        )

    def query_out_copy(g):
        return pltpu.make_async_copy(
            out_ref.at[:, :, group_columns(g)], out_hbm.at[:, :, group_columns(g)], out_sem.at[1, g]
        )

    def give_back(g):
        for d in range(1, reach + 1):

            @pl.when(block >= d)
            def _():
                ret_copy(d, g, block - d).start()

    def one_group(g, sums):
        q_gain_sum, k_gain_sum = sums
        first = pl.multiple_of(g * GROUP_WIDTH, GROUP_WIDTH)
        k_unit, _ = unit(kv_win[g, :, 0:HEAD_SIZE].astype(f32))
        k = (k_unit * k_gain_ref[...]).astype(bf16)
        v = kv_win[g, :, HEAD_SIZE : 2 * HEAD_SIZE]
        k_across = jnp.transpose(k.astype(f32)).astype(bf16)
        v_across = jnp.transpose(v.astype(f32)).astype(bf16)
        for pair in range(GROUP // 2):
            if pair % (GROUP // 4) == 0:
                half = pair // (GROUP // 4)
                raw = packed(2 * g + 2 + half)
                base = pl.multiple_of(first + half * HALF_WIDTH, HALF_WIDTH)
                grads = (
                    grad_ref[0, :, pl.ds(base, HALF_WIDTH)].astype(f32) * advantage
                ).astype(bf16)
            at = pair % (GROUP // 4)
            a = slice(2 * at * HEAD_SIZE, (2 * at + 1) * HEAD_SIZE)
            b = slice((2 * at + 1) * HEAD_SIZE, (2 * at + 2) * HEAD_SIZE)
            across = slice(pair * 2 * tokens, (pair + 1) * 2 * tokens)
            q_unit, q_scale = unit(jnp.concatenate([raw[:, a], raw[:, b]], axis=0))
            q_hat = (q_unit * q_gain_ref[...]).astype(bf16)
            d_out = jnp.concatenate([grads[:, a], grads[:, b]], axis=0)
            score = matmul_last(k, q_hat)
            weight = jnp.exp2(score * (inverse * math.log2(math.e))) * allowed[...]
            total = jnp.sum(weight, axis=0, keepdims=True)
            share = 1.0 / total
            attn = (matmul(v_across, weight.astype(bf16)) * share).astype(bf16).astype(f32)
            delta = jnp.sum(jnp.transpose(d_out.astype(f32)) * attn, axis=0, keepdims=True)
            attn_rows = jnp.transpose(attn).astype(bf16)
            prob = weight * share
            dscore = (prob * (matmul_last(v, d_out) - delta)).astype(bf16)
            prob_s[:, across] = prob.astype(bf16)
            dscore_s[:, across] = dscore
            q_s[across, :] = q_hat
            d_s[across, :] = d_out
            dq_hat = jnp.transpose(matmul(k_across, dscore)) * inverse
            q_gain_sum = q_gain_sum + jnp.sum(dq_hat * q_unit, axis=0, keepdims=True)
            scaled = dq_hat * q_gain_ref[...]
            dq = (
                q_scale * (scaled - q_unit * jnp.mean(scaled * q_unit, axis=-1, keepdims=True))
            ).astype(bf16)
            for i, where in ((0, a), (1, b)):
                cols = pl.ds(pl.multiple_of(base + where.start, HEAD_SIZE), HEAD_SIZE)
                attn_ref[0, :, cols] = attn_rows[i * tokens : (i + 1) * tokens]
                out_ref[0, :, cols] = dq[i * tokens : (i + 1) * tokens]
        dk_part = (matmul(dscore_s[...], q_s[...]) * inverse).astype(bf16)
        part[g, :, 0:HEAD_SIZE] = dk_part
        part[g, :, HEAD_SIZE : 2 * HEAD_SIZE] = matmul(prob_s[...], d_s[...]).astype(bf16)
        @pl.when(g < KEY_VALUE_HEADS - 1)
        def _():
            give_back(g)

        attn_out_copy(g).start()
        query_out_copy(g).start()

        k_gain_sum = k_gain_sum + jnp.sum(dk_part.astype(f32) * k_unit, axis=0, keepdims=True)
        return q_gain_sum, k_gain_sum

    none = jnp.zeros((1, HEAD_SIZE), f32)
    q_gain_sum, k_gain_sum = lax.fori_loop(0, KEY_VALUE_HEADS, one_group, (none, none))

    def gain_copy(buffer, send_sems, recv_sems, axis, home, to, other):
        return pltpu.make_async_remote_copy(
            src_ref=buffer.at[home],
            dst_ref=buffer.at[to],
            send_sem=send_sems.at[other],
            recv_sem=recv_sems.at[to],
            device_id={axis: other},
            device_id_type=MESH,
        )

    over_ctx = functools.partial(gain_copy, gain_ctx, gc_send, gc_recv, "ctx", block)
    over_dp = functools.partial(gain_copy, gain_dp, gd_send, gd_recv, "dp", me)

    def summed(buffer, count):
        total = buffer[0]
        for i in range(1, count):
            total = total + buffer[i]
        return total

    def gain_to(p, q):
        home = me * n_blocks + block
        index, to = device(p, q)
        return pltpu.make_async_remote_copy(
            src_ref=gain_all.at[home],
            dst_ref=gain_all.at[home],
            send_sem=ga_send.at[index],
            recv_sem=ga_recv.at[home],
            device_id=to,
            device_id_type=MESH,
        )

    def gain_from(p, q):
        index, to = device(p, q)
        return pltpu.make_async_remote_copy(
            src_ref=gain_all.at[index],
            dst_ref=gain_all.at[index],
            send_sem=ga_send.at[index],
            recv_sem=ga_recv.at[index],
            device_id=to,
            device_id_type=MESH,
        )

    if everyone:
        gain_all[me * n_blocks + block, 0:1, :] = q_gain_sum
        gain_all[me * n_blocks + block, 1:2, :] = k_gain_sum
        for p, q in others:
            gain_to(p, q).start()
        give_back(KEY_VALUE_HEADS - 1)
    else:
        give_back(KEY_VALUE_HEADS - 1)
        gain_ctx[block, 0:1, :] = q_gain_sum
        gain_ctx[block, 1:2, :] = k_gain_sum
        loop(n_blocks, lambda o: over_ctx(block, beside(o)).start())
        loop(n_blocks, lambda o: over_ctx(beside(o), beside(o)).wait_recv())
        gain_dp[me] = summed(gain_ctx, n_blocks)
        loop(n_ranks, lambda o: over_dp(me, ahead(o)).start())

    def sent_dp(o):
        dest_copy(me, ahead(o), ahead(o)).wait_send()
        for c in range(CHUNKS):
            row_copy(c, ahead(o), me, ahead(o)).wait_send()

    loop(n_ranks, sent_dp)
    for d in range(1, reach + 1):

        @pl.when(block + d < n_blocks)
        def _():
            docs_copy(d, block + d).wait_send()
            kv_copy(d, block + d).wait_send()

        @pl.when(block >= d)
        def _():
            for g in range(KEY_VALUE_HEADS - 1):
                ret_copy(d, g, block - d).wait_send()

    for g in range(KEY_VALUE_HEADS):
        attn_out_copy(g).wait()
        query_out_copy(g).wait()

    for g in range(KEY_VALUE_HEADS):
        for d in range(1, reach + 1):

            @pl.when(block + d < n_blocks)
            def _():
                ret_copy(d, g, block + d).wait_recv()

        both = part[g, 0:tokens, :].astype(f32)
        for d in range(1, reach + 1):
            both = both + ret[d - 1, g].astype(f32)
        k_unit, k_scale = unit(kv_win[g, 0:tokens, 0:HEAD_SIZE].astype(f32))
        scaled = both[:, 0:HEAD_SIZE] * k_gain_ref[...]
        dk = k_scale * (scaled - k_unit * jnp.mean(scaled * k_unit, axis=-1, keepdims=True))
        at = QUERY_WIDTH + g * HEAD_SIZE
        out_ref[0, :, at : at + HEAD_SIZE] = dk.astype(bf16)
        at = at + KEY_WIDTH
        out_ref[0, :, at : at + HEAD_SIZE] = both[:, HEAD_SIZE:].astype(bf16)

    last = pl.ds(QUERY_WIDTH, 2 * KEY_WIDTH)
    last_out = pltpu.make_async_copy(
        out_ref.at[:, :, last], out_hbm.at[:, :, last], out_sem.at[0, KEY_VALUE_HEADS]
    )
    last_out.start()
    if everyone:
        for p, q in others:
            gain_from(p, q).wait_recv()
        gain_ref[0:2, :] = jnp.sum(gain_all[...], axis=0)
    else:
        loop(n_ranks, lambda o: over_dp(ahead(o), ahead(o)).wait_recv())
        gain_ref[...] = summed(gain_dp, n_ranks)
    gain_out = pltpu.make_async_copy(gain_ref, gain_hbm, out_sem.at[1, KEY_VALUE_HEADS])
    gain_out.start()

    for p, q in others:
        gain_to(p, q).wait_send()
    if not everyone:
        loop(n_ranks, lambda o: over_dp(me, ahead(o)).wait_send())
        loop(n_blocks, lambda o: over_ctx(block, beside(o)).wait_send())
    for d in range(1, reach + 1):

        @pl.when(block >= d)
        def _():
            ret_copy(d, KEY_VALUE_HEADS - 1, block - d).wait_send()

    last_out.wait()
    gain_out.wait()


def write_out(attn_in, grads_in, gains, attn, grads, q_sum, k_sum, attn_v, grads_v, gains_v, in_sems, out_sems):
    ways = [(gains, gains_v, gains_v.at[pl.ds(0, 1), :], q_sum)]
    step = attn_in.shape[1] // 4
    for i in range(4):
        rows = (slice(None), pl.ds(i * step, step), slice(None))
        ways.append((attn_in.at[rows], attn_v.at[rows], attn_v.at[rows], attn.at[rows]))
        ways.append((grads_in.at[rows], grads_v.at[rows], grads_v.at[rows], grads.at[rows]))
    come = [pltpu.make_async_copy(w[0], w[1], in_sems.at[i]) for i, w in enumerate(ways)]
    go = [pltpu.make_async_copy(w[2], w[3], out_sems.at[i]) for i, w in enumerate(ways)]
    second = pltpu.make_async_copy(gains_v.at[pl.ds(1, 1), :], k_sum, out_sems.at[len(ways)])
    for copy in come:
        copy.start()
    for i in range(len(ways)):
        come[i].wait()
        go[i].start()
        if i == 0:
            second.start()
    for copy in go:
        copy.wait()
    second.wait()


def per_device(n_ranks, n_blocks, rows, dest_rank, doc_ids, advantage, out_grad, q_gain, k_gain):
    tokens = rows.shape[1]
    width = rows.shape[2]
    reach = min(4, n_blocks - 1)
    capacity = tokens // n_ranks
    pitch = -(-capacity // 16) * 16
    slots = n_ranks * pitch
    keys = (reach + 1) * tokens
    stacked = GROUP * tokens
    direct = n_ranks * n_blocks if n_ranks * n_blocks <= 64 else 1
    dma = pltpu.SemaphoreType.DMA
    hbm = pl.BlockSpec(memory_space=pltpu.HBM)
    results = (
        jax.ShapeDtypeStruct((1, tokens, QUERY_WIDTH), bf16),
        jax.ShapeDtypeStruct((1, tokens, width), bf16),
        jax.ShapeDtypeStruct((1, HEAD_SIZE), f32),
        jax.ShapeDtypeStruct((1, HEAD_SIZE), f32),
    )
    partial = pl.pallas_call(
        functools.partial(kernel, n_ranks, n_blocks, reach, capacity, pitch),
        out_shape=(*results[:2], jax.ShapeDtypeStruct((8, HEAD_SIZE), f32)),
        in_specs=[hbm] * 7,
        out_specs=(hbm,) * 3,
        scratch_shapes=[
            pltpu.VMEM((1, tokens, QUERY_WIDTH), bf16),
            pltpu.VMEM((1, tokens, width), bf16),
            pltpu.VMEM((8, HEAD_SIZE), f32),
            dma((2, KEY_VALUE_HEADS + 1)),
            pltpu.VMEM((CHUNKS, tokens, HALF_WIDTH), bf16),
            pltpu.VMEM((1, tokens), jnp.int32),
            pltpu.VMEM((1, tokens), jnp.int32),
            pltpu.VMEM(advantage.shape, f32),
            pltpu.VMEM((1, tokens, QUERY_WIDTH), bf16),
            pltpu.VMEM((1, HEAD_SIZE), f32),
            pltpu.VMEM((1, HEAD_SIZE), f32),
            dma((6,)),
            dma((CHUNKS,)),
            pltpu.VMEM((n_ranks, 1, tokens), jnp.int32),
            pltpu.VMEM((reach + 1, 1, tokens), jnp.int32),
            pltpu.VMEM((CHUNKS, slots, HALF_WIDTH), bf16),
            pltpu.VMEM((CHUNKS, slots, HALF_WIDTH), bf16),
            pltpu.VMEM((tokens, slots), bf16),
            pltpu.VMEM((KEY_VALUE_HEADS, keys, 2 * HEAD_SIZE), bf16),
            pltpu.VMEM((keys, 2 * tokens), f32),
            pltpu.VMEM((keys, stacked), bf16),
            pltpu.VMEM((keys, stacked), bf16),
            pltpu.VMEM((stacked, HEAD_SIZE), bf16),
            pltpu.VMEM((stacked, HEAD_SIZE), bf16),
            pltpu.VMEM((KEY_VALUE_HEADS, keys, 2 * HEAD_SIZE), bf16),
            pltpu.VMEM((reach, KEY_VALUE_HEADS, tokens, 2 * HEAD_SIZE), bf16),
            pltpu.VMEM((n_blocks, 8, HEAD_SIZE), f32),
            pltpu.VMEM((n_ranks, 8, HEAD_SIZE), f32),
            pltpu.VMEM((direct, 2, HEAD_SIZE), f32),
            dma((n_ranks,)),
            dma((n_ranks,)),
            dma((reach,)),
            dma((reach,)),
            dma((CHUNKS, n_ranks)),
            dma((CHUNKS, n_ranks)),
            dma((reach,)),
            dma((reach,)),
            dma((reach, KEY_VALUE_HEADS)),
            dma((reach, KEY_VALUE_HEADS)),
            dma((n_blocks,)),
            dma((n_blocks,)),
            dma((n_ranks,)),
            dma((n_ranks,)),
            dma((direct,)),
            dma((direct,)),
        ],
        compiler_params=pltpu.CompilerParams(
            collective_id=0, has_side_effects=True, vmem_limit_bytes=62 * 1024 * 1024
        ),
        name="grpo_window",
    )(
        rows,
        dest_rank,
        doc_ids,
        advantage,
        out_grad,
        q_gain.reshape(1, HEAD_SIZE),
        k_gain.reshape(1, HEAD_SIZE),
    )
    attn, grads, q_sum, k_sum = pl.pallas_call(
        write_out,
        out_shape=results,
        in_specs=[hbm] * 3,
        out_specs=(hbm,) * 4,
        scratch_shapes=[
            pltpu.VMEM((1, tokens, QUERY_WIDTH), bf16),
            pltpu.VMEM((1, tokens, width), bf16),
            pltpu.VMEM(partial[2].shape, f32),
            dma((9,)),
            dma((10,)),
        ],
        compiler_params=pltpu.CompilerParams(vmem_limit_bytes=62 * 1024 * 1024),
        name="write_out",
    )(*partial)
    return attn, grads, q_sum.reshape(HEAD_SIZE), k_sum.reshape(HEAD_SIZE)


def solution(mesh):
    placed = (
        P("dp", "ctx", None),
        P("dp", "ctx"),
        P("dp", "ctx"),
        P("dp", None),
        P("dp", "ctx", None),
        P(),
        P(),
    )
    return jax.shard_map(
        functools.partial(per_device, mesh.shape["dp"], mesh.shape["ctx"]),
        mesh=mesh,
        in_specs=placed,
        out_specs=(P("dp", "ctx", None), P("dp", "ctx", None), P(), P()),
        check_vma=False,
    )
```
